32 devices in a mesh: section: 4 (over y, x), expert: 4 (over z), pair: 2 (over core).
Axes of the slice: x: 2, y: 2, z: 4, core: 2. Of those that a mesh axis runs over, the one named last changes fastest.
Arguments:
- initial_state: bfloat16 [2048, 2048], P(('section', 'expert')), may hold values from -6 to 6
- prelude: bfloat16 [2048, 2048], P(('section', 'expert')), may hold values from -6 to 6
- inject_gain: float32 [2048], replicated, may hold values from 0.1 to 1.9
- norm_gain: float32 [2048], replicated, may hold values from 0.1 to 1.9
- router: bfloat16 [2048, 64], replicated, may hold values from -0.125 to 0.125
- gate_w: bfloat16 [64, 2048, 1024], P('expert', 'section', 'pair'), may hold values from -0.125 to 0.125
- up_w: bfloat16 [64, 2048, 1024], P('expert', 'section', 'pair'), may hold values from -0.125 to 0.125
- down_w: bfloat16 [64, 1024, 2048], P('expert', 'pair', 'section'), may hold values from -0.1875 to 0.1875
- routes: int32 [1, 2048, 8], P(None, ('section', 'expert')), may hold values from 0 to 63, all different within a row; in each aligned block of 128 rows (0 to 127, 128 to 255, ..., all dimensions but the last counted through in order) at most 18 rows name the same one
Outputs:
- final_state: bfloat16 [2048, 2048], P(('section', 'expert'), 'pair')
The draws below stay inside these ranges and needn't reach their ends.
Inputs may be any that keep to these rules, and one draw needn't show every extreme that they name: `routes`: each row names 8 different experts. Within the 128 rows of one device in one pass (aligned blocks of the token dimension), no expert is named more than 18 times, a bound that some block reaches.
All inputs are finite; a program needn't handle non-finite values.
Results may differ from the reference program's by a relative error of at most 0.0029.
Values may be sent and summed in bfloat16 or wider, within the bound.
A program may use at most 192 MiB of HBM per device.

```python
import math
import jax
import jax.numpy as jnp
import numpy as np
from jax import lax

D = 2048
HID = 1024
EXPERTS = 64
TOPK = 8
TOK_DEV = 128
LOOPS = 1
CAP = 18
TOKENS = 2048
N_PAIR = 2


def level_of(key, shape, cuts, low, high):
    def one(position, shards_of):
        heights = jax.random.uniform(jax.random.fold_in(jax.random.fold_in(key, 6), position), (shards_of,), jnp.float32, low / len(cuts), high / len(cuts))
        return jnp.repeat(jnp.exp(heights), shape[position] // shards_of).reshape((-1,) + (1,) * (len(shape) - position - 1))

    loudness = one(*cuts[0])
    for cut in cuts[1:]:
        loudness = loudness * one(*cut)
    return loudness


def assign_block(rng, own, number, rows, count, top, reach, skew):
    order = jax.random.permutation(rng, count)
    heavy_load, usual = load_shares(count, rows * top, reach, skew, True), load_shares(count, rows * top, reach, skew, False)
    places = jnp.arange(count)

    def named(sizes, turn):
        used = int((sizes > 0).sum())
        fixed = max(1, used // 4)
        moved = fixed + (places - fixed + turn * (used - fixed)) % max(1, count - fixed)
        return jnp.zeros((count,), jnp.int32).at[order[jnp.where(places < fixed, places, moved)]].set(jnp.asarray(sizes, jnp.int32))

    sizes = jnp.where(number % 4 == 0, named(heavy_load, number // 4), named(usual, number - number // 4 - 1))
    mixed = jax.random.permutation(jax.random.fold_in(own, 3), count)
    source_of, sink = mixed[0:count // 2 * 2:2], mixed[1:count // 2 * 2:2]
    margin = jnp.minimum(sizes[source_of] - 1, reach - sizes[sink]) // 2
    margin = jnp.where((source_of == order[0]) | (sink == order[0]) | (sizes[sink] == 0), 0, jnp.maximum(margin, 0))
    moved = jax.random.randint(jax.random.fold_in(own, 4), (count // 2,), 0, 1 << 20) % (margin + 1)
    sizes = sizes.at[source_of].add(-moved).at[sink].add(moved)
    members = jnp.searchsorted(jnp.cumsum(sizes), jnp.arange(rows * top), side="right").astype(jnp.int32)
    listing = members.reshape(top, rows).T
    listing = listing[jax.random.permutation(jax.random.fold_in(own, 1), rows)]
    turn = jax.random.randint(jax.random.fold_in(own, 2), (rows, 1), 0, top)
    return jnp.take_along_axis(listing, (jnp.arange(top)[None, :] + turn) % top, axis=1)


def load_shares(count, total, bound, lean, full):
    portions = [(1 << 20) // math.isqrt(standing ** lean) + 1 for standing in range(1, count + 1)]
    largest = bound if full else min(bound, max(-(-total // count), total * portions[0] // sum(portions)))
    least = 1 if total - largest >= count - 1 else 0
    counts, spare = [largest] + [least] * (count - 1), total - largest - least * (count - 1)
    while spare > 0:
        movable = [i for i in range(1, count) if counts[i] < largest] or [i for i in range(1, count) if counts[i] < bound]
        pool, budget = sum([portions[i] for i in movable]), spare
        for i in movable:
            extra = min(bound - counts[i], max(1, budget * portions[i] // pool), spare)
            counts[i] = counts[i] + extra
            spare = spare - extra
    return np.array(counts)


def bell_draw(stream_key, shape, width, most, split=(), held_as=jnp.bfloat16):
    array = width * jax.random.normal(stream_key, shape, jnp.float32)
    if split:
        array = array * level_of(stream_key, shape, split, -0.22, 0.18)
    return jnp.clip(array, -most, most).astype(held_as)


def setup_inputs(seed: int = 0) -> dict:
    keys = jax.random.split(jax.random.key(seed), 10)
    initial_state = bell_draw(keys[0], (TOKENS, D), 1.0, 6.0, ((0, 16),))
    prelude = bell_draw(keys[1], (TOKENS, D), 1.0, 6.0, ((0, 16),))
    inject_gain = jnp.clip(1.0 + 0.18 * jax.random.normal(keys[2], (D,), jnp.float32), 0.1, 1.9)
    norm_gain = jnp.clip(1.0 + 0.18 * jax.random.normal(keys[3], (D,), jnp.float32), 0.1, 1.9)
    router = bell_draw(keys[4], (D, EXPERTS), D ** -0.5, 0.125)
    gate_w = bell_draw(keys[5], (EXPERTS, D, HID), D ** -0.5, 0.125, ((0, 4), (1, 4), (2, 2)))
    up_w = bell_draw(keys[6], (EXPERTS, D, HID), D ** -0.5, 0.125, ((0, 4), (1, 4), (2, 2)))
    down_w = bell_draw(keys[7], (EXPERTS, HID, D), HID ** -0.5, 0.1875, ((0, 4), (1, 2), (2, 4)))
    routes_keys = jax.random.split(jax.random.fold_in(keys[8], 1), LOOPS * TOKENS // TOK_DEV)
    routes_turns = jax.random.permutation(jax.random.fold_in(keys[8], 3), LOOPS * TOKENS // TOK_DEV)
    routes = jax.vmap(lambda own, number: assign_block(jax.random.fold_in(keys[8], 2), own, number, TOK_DEV, EXPERTS, TOPK, CAP, 2))(routes_keys, routes_turns).reshape((LOOPS, TOKENS, TOPK))
    return {"initial_state": initial_state, "prelude": prelude, "inject_gain": inject_gain, "norm_gain": norm_gain, "router": router, "gate_w": gate_w, "up_w": up_w, "down_w": down_w, "routes": routes}


def reference(initial_state, prelude, inject_gain, norm_gain, router, gate_w, up_w, down_w, routes):
    hidden_state = initial_state.astype(jnp.float32)
    prelude_f = prelude.astype(jnp.float32)
    block_count = TOKENS // TOK_DEV
    half_width = HID // N_PAIR
    token_ids = jnp.broadcast_to(jnp.arange(TOKENS, dtype=jnp.int32).reshape(block_count, TOK_DEV, 1), (block_count, TOK_DEV, TOPK)).reshape(-1)
    block_ids = jnp.broadcast_to(jnp.arange(block_count, dtype=jnp.int32)[:, None], (block_count, TOK_DEV * TOPK))
    for pass_index in range(LOOPS):
        mixed_state = hidden_state + prelude_f * inject_gain
        inv_rms = lax.rsqrt(lax.optimization_barrier(jnp.mean(mixed_state * mixed_state, axis=-1, keepdims=True)) + 1e-06)
        normed = (mixed_state * inv_rms * norm_gain).astype(jnp.bfloat16)
        logits = jnp.dot(normed, router, preferred_element_type=jnp.float32)
        router_prob = jax.nn.sigmoid(logits)
        chosen = routes[pass_index]
        picked = jnp.take_along_axis(router_prob, chosen, axis=1)
        gate_vals = picked / lax.optimization_barrier(jnp.sum(picked, axis=1, keepdims=True))
        flat_ids = chosen.reshape(block_count, TOK_DEV * TOPK)
        onehot = (flat_ids[:, :, None] == jnp.arange(EXPERTS, dtype=jnp.int32)).astype(jnp.int32)
        before = jnp.cumsum(onehot, axis=1) - onehot
        slot_rank = lax.optimization_barrier(jnp.sum(before * onehot, axis=-1))
        column = (block_ids * CAP + slot_rank).reshape(-1).astype(jnp.int32)
        expert_ids = flat_ids.reshape(-1).astype(jnp.int32)
        slot_table = jnp.full((EXPERTS, block_count * CAP), TOKENS, jnp.int32).at[expert_ids, column].set(token_ids)
        weight_table = jnp.zeros((EXPERTS, block_count * CAP), jnp.float32).at[expert_ids, column].set(gate_vals.reshape(-1))
        padded_rows = jnp.concatenate([normed, jnp.zeros((1, D), jnp.bfloat16)], axis=0)

        def one_expert(moe_total, expert_items):
            slot_row, weight_row, gate_one, up_one, down_one = expert_items
            row_block = padded_rows[slot_row]
            gate_act = jnp.dot(row_block, gate_one, preferred_element_type=jnp.float32)
            up_act = jnp.dot(row_block, up_one, preferred_element_type=jnp.float32)
            inner_act = (jax.nn.silu(gate_act) * up_act).astype(jnp.bfloat16)
            result = jnp.zeros((row_block.shape[0], D), jnp.float32)
            for half_index in range(N_PAIR):
                half_part = jnp.dot(inner_act[:, half_index * half_width:(half_index + 1) * half_width], down_one[half_index * half_width:(half_index + 1) * half_width], preferred_element_type=jnp.float32).astype(jnp.bfloat16)
                result = result + half_part.astype(jnp.float32)
            result = result.astype(jnp.bfloat16).astype(jnp.float32)
            moe_total = moe_total.at[slot_row].add(weight_row[:, None] * result, mode='drop')
            return (moe_total, None)
        moe_out = lax.scan(one_expert, jnp.zeros((TOKENS, D), jnp.float32), (slot_table, weight_table, gate_w, up_w, down_w))[0]
        hidden_state = mixed_state + moe_out
    return hidden_state.astype(jnp.bfloat16)
```

```python
import jax
import jax.numpy as jnp
from jax import lax
from jax.sharding import PartitionSpec as P

TOPK = 8
CAP = 18


def gather_weights(initial_state, prelude, inject_gain, norm_gain, router, gate_w, up_w, down_w, routes):
    gate_full, up_full, down_full = (
        lax.all_gather(gate_w, "section", axis=1, tiled=True),
        lax.all_gather(up_w, "section", axis=1, tiled=True),
        lax.all_gather(down_w, "section", axis=2, tiled=True),
    )
    paired_w = jnp.concatenate([gate_full, up_full], axis=2)
    local_count = gate_full.shape[0]
    half_width = gate_full.shape[2]
    tok_count, model_width = initial_state.shape
    experts_all = router.shape[1]
    pair_count = lax.axis_size("pair")
    pair_pos = lax.axis_index("pair")
    part_width = model_width // pair_count
    hidden_state = initial_state.astype(jnp.float32)
    prelude_f = prelude.astype(jnp.float32)
    token_ids = jnp.broadcast_to(
        jnp.arange(tok_count, dtype=jnp.int32)[:, None], (tok_count, TOPK)
    ).reshape(-1)
    expert_range = jnp.arange(experts_all, dtype=jnp.int32)
    mixed_state = hidden_state + prelude_f * inject_gain
    inv_rms = lax.rsqrt(jnp.mean(mixed_state * mixed_state, axis=-1, keepdims=True) + 1e-06)
    normed = (mixed_state * inv_rms * norm_gain).astype(jnp.bfloat16)
    logits = jnp.dot(normed, router, preferred_element_type=jnp.float32)
    router_prob = jax.nn.sigmoid(logits)
    chosen = routes[0]
    onehot_k = (chosen[:, :, None] == expert_range).astype(jnp.float32)
    picked = jnp.sum(onehot_k * router_prob[:, None, :], axis=-1)
    gate_vals = picked / jnp.sum(picked, axis=1, keepdims=True)
    flat_ids = chosen.reshape(-1)
    onehot = (flat_ids[:, None] == expert_range).astype(jnp.bfloat16)
    order = jnp.arange(flat_ids.shape[0], dtype=jnp.int32)
    earlier = (order[:, None] > order[None, :]).astype(jnp.bfloat16)
    before = jnp.dot(earlier, onehot, preferred_element_type=jnp.float32)
    slot_rank = jnp.sum(before * onehot.astype(jnp.float32), axis=-1).astype(jnp.int32)
    slot_ids = flat_ids * CAP + slot_rank
    source_rows = jnp.full((experts_all * CAP,), tok_count, jnp.int32).at[slot_ids].set(token_ids)
    padded_rows = jnp.concatenate([normed, jnp.zeros((1, model_width), jnp.bfloat16)], axis=0)
    outgoing = padded_rows[source_rows].reshape(experts_all, CAP, padded_rows.shape[1])
    received = lax.all_to_all(outgoing, "expert", split_axis=0, concat_axis=0, tiled=True)
    slot_count = received.shape[1]
    grouped = received.reshape(-1, local_count, slot_count, model_width)
    gate_up = jnp.einsum("sekd,edh->sekh", grouped, paired_w, preferred_element_type=jnp.float32)
    inner_act = (jax.nn.silu(gate_up[..., :half_width]) * gate_up[..., half_width:]).astype(
        jnp.bfloat16
    )
    partial_out = jnp.einsum(
        "sekh,ehd->sekd", inner_act, down_full, preferred_element_type=jnp.float32
    ).astype(jnp.bfloat16)
    lead = partial_out.shape[0]
    pieces = jnp.moveaxis(
        partial_out.reshape(lead, local_count, slot_count, pair_count, part_width), 3, 0
    )
    arrived = lax.all_to_all(pieces, "pair", split_axis=0, concat_axis=0, tiled=True)
    summed = jnp.sum(arrived.astype(jnp.float32), axis=0).astype(jnp.bfloat16)
    returned_rows = lax.all_to_all(
        summed.reshape(-1, slot_count, summed.shape[-1]),
        "expert",
        split_axis=0,
        concat_axis=0,
        tiled=True,
    )
    back_width = returned_rows.shape[-1]
    flat_back = returned_rows.reshape(experts_all * CAP, back_width)
    taken_rows = flat_back[slot_ids].reshape(tok_count, TOPK, back_width)
    moe_out = jnp.sum(gate_vals[:, :, None] * taken_rows.astype(jnp.float32), axis=1)
    hidden_state = (
        lax.dynamic_slice_in_dim(mixed_state, pair_pos * part_width, part_width, 1) + moe_out
    )
    return hidden_state.astype(jnp.bfloat16)


def move_tokens(initial_state, prelude, inject_gain, norm_gain, router, gate_w, up_w, down_w, routes):
    sections, zs, pairs = (lax.axis_size(a) for a in ("section", "expert", "pair"))
    pair_pos = lax.axis_index("pair")
    local_count, depth, _ = gate_w.shape
    tok_count, model_width = initial_state.shape
    experts_all = router.shape[1]
    part_width = model_width // pairs
    slots = CAP * zs
    sec_toks = zs * tok_count

    all_routes = lax.all_gather(routes[0], ("section", "expert"), axis=0, tiled=True)
    all_routes = all_routes.reshape(sections, sec_toks, TOPK)

    mixed = initial_state.astype(jnp.float32) + prelude.astype(jnp.float32) * inject_gain
    inv_rms = lax.rsqrt(jnp.mean(mixed * mixed, axis=-1, keepdims=True) + 1e-06)
    normed = (mixed * inv_rms * norm_gain).astype(jnp.bfloat16)

    half_toks = tok_count // pairs
    mine = lax.dynamic_slice_in_dim(normed, pair_pos * half_toks, half_toks, 0)
    sliced = lax.all_to_all(mine, "section", split_axis=1, concat_axis=0, tiled=True)
    rows = lax.all_gather(sliced, ("expert", "pair"), axis=0, tiled=False)
    rows = rows.reshape(zs, pairs, sections, half_toks, depth)
    rows = rows.transpose(2, 0, 1, 3, 4).reshape(sections, sec_toks, depth)

    logits = jnp.dot(normed, router, preferred_element_type=jnp.float32)
    prob = jax.nn.sigmoid(logits)
    onehot_k = (routes[0][:, :, None] == jnp.arange(experts_all, dtype=jnp.int32)).astype(jnp.float32)
    picked = jnp.sum(onehot_k * prob[:, None, :], axis=-1)
    gates = picked / jnp.sum(picked, axis=1, keepdims=True)
    all_gates = lax.all_gather(gates, ("section", "expert"), axis=0, tiled=True)
    all_gates = all_gates.reshape(sections, sec_toks, TOPK)

    first = lax.axis_index("expert") * local_count
    own = first + jnp.arange(local_count, dtype=jnp.int32)
    hits = all_routes[:, None, :, :] == own[None, :, None, None]
    member = jnp.any(hits, axis=-1)
    member_gate = jnp.sum(jnp.where(hits, all_gates[:, None, :, :], 0.0), axis=-1)
    order = jnp.arange(sec_toks, dtype=jnp.int32)
    earlier = (order[:, None] < order[None, :]).astype(jnp.bfloat16)
    rank = jnp.einsum(
        "seu,ut->set", member.astype(jnp.bfloat16), earlier, preferred_element_type=jnp.float32
    )
    place = jnp.where(member, rank, -1.0).astype(jnp.int32)
    at_slot = place[:, :, None, :] == jnp.arange(slots, dtype=jnp.int32)[:, None]
    dispatch = at_slot.astype(jnp.bfloat16)
    combine = jnp.where(at_slot, member_gate[:, :, None, :], 0.0).astype(jnp.bfloat16)

    grouped = jnp.einsum(
        "sect,std->secd", dispatch, rows, preferred_element_type=jnp.float32
    ).astype(jnp.bfloat16)

    def product(weight):
        part = jnp.einsum(
            "secd,edh->sech", grouped, weight, preferred_element_type=jnp.float32
        ).astype(jnp.bfloat16)
        parts = lax.all_to_all(part, "section", split_axis=0, concat_axis=0, tiled=True)
        return jnp.sum(parts.astype(jnp.float32), axis=0)

    act = (jax.nn.silu(product(gate_w)) * product(up_w)).astype(jnp.bfloat16)
    all_act = lax.all_gather(act, "section", axis=0, tiled=False)
    outs = jnp.einsum(
        "sech,ehd->secd", all_act, down_w, preferred_element_type=jnp.float32
    ).astype(jnp.bfloat16)
    moe = jnp.einsum("sect,secd->std", combine, outs, preferred_element_type=jnp.float32)

    fine = depth // pairs
    moe = moe.astype(jnp.bfloat16).reshape(sections, zs, tok_count, pairs, fine)
    moe = lax.all_to_all(moe.transpose(3, 1, 0, 2, 4), "pair", split_axis=0, concat_axis=0, tiled=True)
    moe = jnp.sum(moe.astype(jnp.float32), axis=0).astype(jnp.bfloat16)
    moe = lax.all_to_all(moe, "expert", split_axis=0, concat_axis=0, tiled=True)
    moe = jnp.sum(moe.astype(jnp.float32), axis=0).astype(jnp.bfloat16)
    moe = lax.all_to_all(moe, "section", split_axis=0, concat_axis=0, tiled=True)
    moe = moe.reshape(pairs, sections // pairs, tok_count, fine)
    moe = lax.all_to_all(moe, "pair", split_axis=0, concat_axis=0, tiled=True)
    moe = moe.transpose(2, 1, 0, 3).reshape(tok_count, part_width)
    state = lax.dynamic_slice_in_dim(mixed, pair_pos * part_width, part_width, 1)
    return (state + moe.astype(jnp.float32)).astype(jnp.bfloat16)


def on_device(initial_state, prelude, inject_gain, norm_gain, router, gate_w, up_w, down_w, routes):
    sections, zs, pairs = (lax.axis_size(a) for a in ("section", "expert", "pair"))
    slot_bytes = 2 * sections * gate_w.shape[0] * CAP * zs * zs * initial_state.shape[0]
    fits = slot_bytes <= 16 * 2**20 and sections % pairs == 0 and initial_state.shape[0] % pairs == 0
    plan = move_tokens if fits else gather_weights
    return plan(
        initial_state, prelude, inject_gain, norm_gain, router, gate_w, up_w, down_w, routes
    )


def solution(mesh):
    placed = (
        P(("section", "expert"), None),
        P(("section", "expert"), None),
        P(),
        P(),
        P(),
        P("expert", "section", "pair"),
        P("expert", "section", "pair"),
        P("expert", "pair", "section"),
        P(None, ("section", "expert"), None),
    )
    return jax.shard_map(
        on_device,
        mesh=mesh,
        in_specs=placed,
        out_specs=P(("section", "expert"), "pair"),
        check_vma=False,
    )
```

```python
import jax
import jax.numpy as jnp
from jax import lax
from jax.sharding import PartitionSpec as P

TOPK = 8
CAP = 18


def gather_weights(initial_state, prelude, inject_gain, norm_gain, router, gate_w, up_w, down_w, routes):
    gate_full, up_full, down_full = (
        lax.all_gather(gate_w, "section", axis=1, tiled=True),
        lax.all_gather(up_w, "section", axis=1, tiled=True),
        lax.all_gather(down_w, "section", axis=2, tiled=True),
    )
    paired_w = jnp.concatenate([gate_full, up_full], axis=2)
    local_count = gate_full.shape[0]
    half_width = gate_full.shape[2]
    tok_count, model_width = initial_state.shape
    experts_all = router.shape[1]
    pair_count = lax.axis_size("pair")
    pair_pos = lax.axis_index("pair")
    part_width = model_width // pair_count
    hidden_state = initial_state.astype(jnp.float32)
    prelude_f = prelude.astype(jnp.float32)
    token_ids = jnp.broadcast_to(
        jnp.arange(tok_count, dtype=jnp.int32)[:, None], (tok_count, TOPK)
    ).reshape(-1)
    expert_range = jnp.arange(experts_all, dtype=jnp.int32)
    mixed_state = hidden_state + prelude_f * inject_gain
    inv_rms = lax.rsqrt(jnp.mean(mixed_state * mixed_state, axis=-1, keepdims=True) + 1e-06)
    normed = (mixed_state * inv_rms * norm_gain).astype(jnp.bfloat16)
    logits = jnp.dot(normed, router, preferred_element_type=jnp.float32)
    router_prob = jax.nn.sigmoid(logits)
    chosen = routes[0]
    onehot_k = (chosen[:, :, None] == expert_range).astype(jnp.float32)
    picked = jnp.sum(onehot_k * router_prob[:, None, :], axis=-1)
    gate_vals = picked / jnp.sum(picked, axis=1, keepdims=True)
    flat_ids = chosen.reshape(-1)
    onehot = (flat_ids[:, None] == expert_range).astype(jnp.bfloat16)
    order = jnp.arange(flat_ids.shape[0], dtype=jnp.int32)
    earlier = (order[:, None] > order[None, :]).astype(jnp.bfloat16)
    before = jnp.dot(earlier, onehot, preferred_element_type=jnp.float32)
    slot_rank = jnp.sum(before * onehot.astype(jnp.float32), axis=-1).astype(jnp.int32)
    slot_ids = flat_ids * CAP + slot_rank
    source_rows = jnp.full((experts_all * CAP,), tok_count, jnp.int32).at[slot_ids].set(token_ids)
    padded_rows = jnp.concatenate([normed, jnp.zeros((1, model_width), jnp.bfloat16)], axis=0)
    outgoing = padded_rows[source_rows].reshape(experts_all, CAP, padded_rows.shape[1])
    received = lax.all_to_all(outgoing, "expert", split_axis=0, concat_axis=0, tiled=True)
    slot_count = received.shape[1]
    grouped = received.reshape(-1, local_count, slot_count, model_width)
    gate_up = jnp.einsum("sekd,edh->sekh", grouped, paired_w, preferred_element_type=jnp.float32)
    inner_act = (jax.nn.silu(gate_up[..., :half_width]) * gate_up[..., half_width:]).astype(
        jnp.bfloat16
    )
    partial_out = jnp.einsum(
        "sekh,ehd->sekd", inner_act, down_full, preferred_element_type=jnp.float32
    ).astype(jnp.bfloat16)
    lead = partial_out.shape[0]
    pieces = jnp.moveaxis(
        partial_out.reshape(lead, local_count, slot_count, pair_count, part_width), 3, 0
    )
    arrived = lax.all_to_all(pieces, "pair", split_axis=0, concat_axis=0, tiled=True)
    summed = jnp.sum(arrived.astype(jnp.float32), axis=0).astype(jnp.bfloat16)
    returned_rows = lax.all_to_all(
        summed.reshape(-1, slot_count, summed.shape[-1]),
        "expert",
        split_axis=0,
        concat_axis=0,
        tiled=True,
    )
    back_width = returned_rows.shape[-1]
    flat_back = returned_rows.reshape(experts_all * CAP, back_width)
    taken_rows = flat_back[slot_ids].reshape(tok_count, TOPK, back_width)
    moe_out = jnp.sum(gate_vals[:, :, None] * taken_rows.astype(jnp.float32), axis=1)
    hidden_state = (
        lax.dynamic_slice_in_dim(mixed_state, pair_pos * part_width, part_width, 1) + moe_out
    )
    return hidden_state.astype(jnp.bfloat16)


def move_tokens(initial_state, prelude, inject_gain, norm_gain, router, gate_w, up_w, down_w, routes):
    sections, zs, pairs = (lax.axis_size(a) for a in ("section", "expert", "pair"))
    me, z, pair_pos = (lax.axis_index(a) for a in ("section", "expert", "pair"))
    local_count, depth, _ = gate_w.shape
    tok_count, model_width = initial_state.shape
    experts_all = router.shape[1]
    part_width = model_width // pairs
    slots = CAP * zs
    sec_toks = zs * tok_count
    half_toks = tok_count // pairs
    first_core = pair_pos == 0

    def to_section(x, j):
        return lax.ppermute(x, "section", [(s, s ^ j) for s in range(sections)])

    def to_lower(x, k):
        return lax.ppermute(x, "expert", [(i, (i - k) % zs) for i in range(zs)])

    def to_upper(x, k):
        return lax.ppermute(x, "expert", [(i, (i + k) % zs) for i in range(zs)])

    def to_other_core(x):
        return lax.ppermute(x, "pair", [(0, 1), (1, 0)])

    mixed = initial_state.astype(jnp.float32) + prelude.astype(jnp.float32) * inject_gain
    inv_rms = lax.rsqrt(jnp.mean(mixed * mixed, axis=-1, keepdims=True) + 1e-06)
    normed = (mixed * inv_rms * norm_gain).astype(jnp.bfloat16)

    mine = lax.dynamic_slice_in_dim(normed, pair_pos * half_toks, half_toks, 0)
    sliced = []
    for j in range(sections):
        piece = lax.dynamic_slice_in_dim(mine, (me ^ j) * depth, depth, 1)
        sliced.append(piece if j == 0 else to_section(piece, j))
    sliced = jnp.stack(sliced)
    half = jnp.stack([sliced if k == 0 else to_upper(sliced, k) for k in range(zs)], axis=1)
    other = to_other_core(half)
    rows = jnp.where(
        first_core, jnp.stack([half, other], axis=2), jnp.stack([other, half], axis=2)
    ).reshape(sections, sec_toks, depth)

    logits = jnp.dot(normed, router, preferred_element_type=jnp.float32)
    prob = jax.nn.sigmoid(logits)
    onehot_k = (routes[0][:, :, None] == jnp.arange(experts_all, dtype=jnp.int32)).astype(jnp.float32)
    picked = jnp.sum(onehot_k * prob[:, None, :], axis=-1)
    gates = picked / jnp.sum(picked, axis=1, keepdims=True)
    table = jnp.concatenate([routes[0].astype(jnp.float32), gates], axis=1)
    table = lax.all_gather(table, ("section", "expert"), axis=0, tiled=False)
    table = table.reshape(sections, zs, tok_count, 2 * TOPK)
    table = jnp.stack([lax.dynamic_index_in_dim(table, me ^ j, 0, False) for j in range(sections)])
    table = jnp.stack(
        [lax.dynamic_index_in_dim(table, lax.rem(z + zs - k, zs), 1, False) for k in range(zs)], axis=1
    )
    table = table.reshape(sections, sec_toks, 2 * TOPK)
    all_routes, all_gates = table[..., :TOPK].astype(jnp.int32), table[..., TOPK:]

    own = z * local_count + jnp.arange(local_count, dtype=jnp.int32)
    hits = all_routes[:, None, :, :] == own[None, :, None, None]
    member = jnp.any(hits, axis=-1)
    member_gate = jnp.sum(jnp.where(hits, all_gates[:, None, :, :], 0.0), axis=-1)
    order = jnp.arange(sec_toks, dtype=jnp.int32)
    earlier = (order[:, None] < order[None, :]).astype(jnp.bfloat16)
    rank = jnp.einsum(
        "seu,ut->set", member.astype(jnp.bfloat16), earlier, preferred_element_type=jnp.float32
    )
    place = jnp.where(member, rank, -1.0).astype(jnp.int32)
    at_slot = place[:, :, None, :] == jnp.arange(slots, dtype=jnp.int32)[:, None]
    dispatch = at_slot.astype(jnp.bfloat16)
    combine = jnp.where(at_slot, member_gate[:, :, None, :], 0.0).astype(jnp.bfloat16)

    grouped = jnp.einsum(
        "sect,std->secd", dispatch, rows, preferred_element_type=jnp.float32
    ).astype(jnp.bfloat16)

    def product(a, b, weight):
        x = jnp.concatenate([grouped[a], grouped[b]], axis=1)
        return jnp.einsum("ecd,edh->ech", x, weight, preferred_element_type=jnp.float32)

    def summed(weight, near, far):
        got = to_section(product(near, 3, weight).astype(jnp.bfloat16), near)
        both = product(0, far, weight) + got.astype(jnp.float32)
        got = to_section(both[:, slots:].astype(jnp.bfloat16), far)
        return both[:, :slots] + got.astype(jnp.float32)

    act = (jax.nn.silu(summed(gate_w, 1, 2)) * summed(up_w, 2, 1)).astype(jnp.bfloat16)

    act1, act2 = to_section(act, 1), to_section(act, 2)
    cut = local_count // 2
    act3 = (to_section(act1[:cut], 2), to_section(act2[cut:], 1))

    def gated_sum(j, a, lo, hi):
        out = jnp.einsum(
            "ech,ehd->ecd", a, down_w[lo:hi], preferred_element_type=jnp.float32
        ).astype(jnp.bfloat16)
        return jnp.einsum(
            "ect,ecd->td", combine[j, lo:hi], out, preferred_element_type=jnp.float32
        )

    def deliver(low, high, shift):
        low, high = (b.astype(jnp.bfloat16).reshape(zs, tok_count, depth) for b in (low, high))
        got = to_other_core(jnp.where(first_core, high, low))
        kept = jnp.where(first_core, low, high)
        both = (kept.astype(jnp.float32) + got.astype(jnp.float32)).astype(jnp.bfloat16)
        total = both[0].astype(jnp.float32)
        for k in range(1, zs):
            total = total + to_lower(both[k], k).astype(jnp.float32)
        moves = []
        for s in range(sections):
            for p in range(pairs):
                moves.append((s * pairs + p, (s ^ (shift + 2 * p)) * pairs + s // 2))
        return lax.ppermute(total.astype(jnp.bfloat16), ("section", "pair"), moves)

    block0 = gated_sum(0, act, 0, local_count)
    block1 = gated_sum(1, act1, 0, local_count)
    block2 = gated_sum(2, act2, 0, local_count)
    same = deliver(block0, block2, 0)
    block3 = gated_sum(3, act3[0], 0, cut) + gated_sum(3, act3[1], cut, local_count)
    unlike = deliver(block1, block3, 1)
    moe = jnp.where(
        me % 2 == 0,
        jnp.concatenate([same, unlike], axis=1),
        jnp.concatenate([unlike, same], axis=1),
    )
    state = lax.dynamic_slice_in_dim(mixed, pair_pos * part_width, part_width, 1)
    return (state + moe.astype(jnp.float32)).astype(jnp.bfloat16)


def on_device(initial_state, prelude, inject_gain, norm_gain, router, gate_w, up_w, down_w, routes):
    sections, zs, pairs = (lax.axis_size(a) for a in ("section", "expert", "pair"))
    slot_bytes = 2 * sections * gate_w.shape[0] * CAP * zs * zs * initial_state.shape[0]
    fits = slot_bytes <= 16 * 2**20 and sections == 4 and pairs == 2
    plan = move_tokens if fits else gather_weights
    return plan(
        initial_state, prelude, inject_gain, norm_gain, router, gate_w, up_w, down_w, routes
    )


def solution(mesh):
    placed = (
        P(("section", "expert"), None),
        P(("section", "expert"), None),
        P(),
        P(),
        P(),
        P("expert", "section", "pair"),
        P("expert", "section", "pair"),
        P("expert", "pair", "section"),
        P(None, ("section", "expert"), None),
    )
    return jax.shard_map(
        on_device,
        mesh=mesh,
        in_specs=placed,
        out_specs=P(("section", "expert"), "pair"),
        check_vma=False,
    )
```

```python
import jax
import jax.numpy as jnp
from jax import lax
from jax.sharding import PartitionSpec as P

TOPK = 8
CAP = 18


def gather_weights(initial_state, prelude, inject_gain, norm_gain, router, gate_w, up_w, down_w, routes):
    gate_full, up_full, down_full = (
        lax.all_gather(gate_w, "section", axis=1, tiled=True),
        lax.all_gather(up_w, "section", axis=1, tiled=True),
        lax.all_gather(down_w, "section", axis=2, tiled=True),
    )
    paired_w = jnp.concatenate([gate_full, up_full], axis=2)
    local_count = gate_full.shape[0]
    half_width = gate_full.shape[2]
    tok_count, model_width = initial_state.shape
    experts_all = router.shape[1]
    pair_count = lax.axis_size("pair")
    pair_pos = lax.axis_index("pair")
    part_width = model_width // pair_count
    hidden_state = initial_state.astype(jnp.float32)
    prelude_f = prelude.astype(jnp.float32)
    token_ids = jnp.broadcast_to(
        jnp.arange(tok_count, dtype=jnp.int32)[:, None], (tok_count, TOPK)
    ).reshape(-1)
    expert_range = jnp.arange(experts_all, dtype=jnp.int32)
    mixed_state = hidden_state + prelude_f * inject_gain
    inv_rms = lax.rsqrt(jnp.mean(mixed_state * mixed_state, axis=-1, keepdims=True) + 1e-06)
    normed = (mixed_state * inv_rms * norm_gain).astype(jnp.bfloat16)
    logits = jnp.dot(normed, router, preferred_element_type=jnp.float32)
    router_prob = jax.nn.sigmoid(logits)
    chosen = routes[0]
    onehot_k = (chosen[:, :, None] == expert_range).astype(jnp.float32)
    picked = jnp.sum(onehot_k * router_prob[:, None, :], axis=-1)
    gate_vals = picked / jnp.sum(picked, axis=1, keepdims=True)
    flat_ids = chosen.reshape(-1)
    onehot = (flat_ids[:, None] == expert_range).astype(jnp.bfloat16)
    order = jnp.arange(flat_ids.shape[0], dtype=jnp.int32)
    earlier = (order[:, None] > order[None, :]).astype(jnp.bfloat16)
    before = jnp.dot(earlier, onehot, preferred_element_type=jnp.float32)
    slot_rank = jnp.sum(before * onehot.astype(jnp.float32), axis=-1).astype(jnp.int32)
    slot_ids = flat_ids * CAP + slot_rank
    source_rows = jnp.full((experts_all * CAP,), tok_count, jnp.int32).at[slot_ids].set(token_ids)
    padded_rows = jnp.concatenate([normed, jnp.zeros((1, model_width), jnp.bfloat16)], axis=0)
    outgoing = padded_rows[source_rows].reshape(experts_all, CAP, padded_rows.shape[1])
    received = lax.all_to_all(outgoing, "expert", split_axis=0, concat_axis=0, tiled=True)
    slot_count = received.shape[1]
    grouped = received.reshape(-1, local_count, slot_count, model_width)
    gate_up = jnp.einsum("sekd,edh->sekh", grouped, paired_w, preferred_element_type=jnp.float32)
    inner_act = (jax.nn.silu(gate_up[..., :half_width]) * gate_up[..., half_width:]).astype(
        jnp.bfloat16
    )
    partial_out = jnp.einsum(
        "sekh,ehd->sekd", inner_act, down_full, preferred_element_type=jnp.float32
    ).astype(jnp.bfloat16)
    lead = partial_out.shape[0]
    pieces = jnp.moveaxis(
        partial_out.reshape(lead, local_count, slot_count, pair_count, part_width), 3, 0
    )
    arrived = lax.all_to_all(pieces, "pair", split_axis=0, concat_axis=0, tiled=True)
    summed = jnp.sum(arrived.astype(jnp.float32), axis=0).astype(jnp.bfloat16)
    returned_rows = lax.all_to_all(
        summed.reshape(-1, slot_count, summed.shape[-1]),
        "expert",
        split_axis=0,
        concat_axis=0,
        tiled=True,
    )
    back_width = returned_rows.shape[-1]
    flat_back = returned_rows.reshape(experts_all * CAP, back_width)
    taken_rows = flat_back[slot_ids].reshape(tok_count, TOPK, back_width)
    moe_out = jnp.sum(gate_vals[:, :, None] * taken_rows.astype(jnp.float32), axis=1)
    hidden_state = (
        lax.dynamic_slice_in_dim(mixed_state, pair_pos * part_width, part_width, 1) + moe_out
    )
    return hidden_state.astype(jnp.bfloat16)


def move_tokens(initial_state, prelude, inject_gain, norm_gain, router, gate_w, up_w, down_w, routes):
    sections, zs, pairs = (lax.axis_size(a) for a in ("section", "expert", "pair"))
    me, z, pair_pos = (lax.axis_index(a) for a in ("section", "expert", "pair"))
    local_count, depth, _ = gate_w.shape
    tok_count, model_width = initial_state.shape
    experts_all = router.shape[1]
    part_width = model_width // pairs
    slots = CAP * zs
    sec_toks = zs * tok_count
    half_toks = tok_count // pairs
    first_core = pair_pos == 0

    def to_section(x, j):
        return lax.ppermute(x, "section", [(s, s ^ j) for s in range(sections)])

    def to_lower(x, k):
        return lax.ppermute(x, "expert", [(i, (i - k) % zs) for i in range(zs)])

    def to_upper(x, k):
        return lax.ppermute(x, "expert", [(i, (i + k) % zs) for i in range(zs)])

    def to_other_core(x):
        return lax.ppermute(x, "pair", [(0, 1), (1, 0)])

    mixed = initial_state.astype(jnp.float32) + prelude.astype(jnp.float32) * inject_gain
    inv_rms = lax.rsqrt(jnp.mean(mixed * mixed, axis=-1, keepdims=True) + 1e-06)
    normed = (mixed * inv_rms * norm_gain).astype(jnp.bfloat16)

    mine = lax.dynamic_slice_in_dim(normed, pair_pos * half_toks, half_toks, 0)
    sliced = []
    for j in range(sections):
        piece = lax.dynamic_slice_in_dim(mine, (me ^ j) * depth, depth, 1)
        sliced.append(piece if j == 0 else to_section(piece, j))
    sliced = jnp.stack(sliced)
    half = jnp.stack([sliced if k == 0 else to_upper(sliced, k) for k in range(zs)], axis=1)
    other = to_other_core(half)
    rows = jnp.where(
        first_core, jnp.stack([half, other], axis=2), jnp.stack([other, half], axis=2)
    ).reshape(sections, sec_toks, depth)

    logits = jnp.dot(normed, router, preferred_element_type=jnp.float32)
    prob = jax.nn.sigmoid(logits)
    onehot_k = (routes[0][:, :, None] == jnp.arange(experts_all, dtype=jnp.int32)).astype(jnp.float32)
    picked = jnp.sum(onehot_k * prob[:, None, :], axis=-1)
    gates = picked / jnp.sum(picked, axis=1, keepdims=True)
    table = jnp.concatenate([routes[0].astype(jnp.float32), gates], axis=1).T
    table = jnp.stack([table if j == 0 else to_section(table, j) for j in range(sections)])
    table = jnp.stack([table if k == 0 else to_upper(table, k) for k in range(zs)], axis=1)
    table = table.transpose(0, 1, 3, 2).reshape(sections, sec_toks, 2 * TOPK)
    all_routes, all_gates = table[..., :TOPK].astype(jnp.int32), table[..., TOPK:]

    own = z * local_count + jnp.arange(local_count, dtype=jnp.int32)
    hits = all_routes[:, None, :, :] == own[None, :, None, None]
    member = jnp.any(hits, axis=-1)
    member_gate = jnp.sum(jnp.where(hits, all_gates[:, None, :, :], 0.0), axis=-1)
    order = jnp.arange(sec_toks, dtype=jnp.int32)
    earlier = (order[:, None] < order[None, :]).astype(jnp.bfloat16)
    rank = jnp.einsum(
        "seu,ut->set", member.astype(jnp.bfloat16), earlier, preferred_element_type=jnp.float32
    )
    place = jnp.where(member, rank, -1.0).astype(jnp.int32)
    at_slot = place[:, :, None, :] == jnp.arange(slots, dtype=jnp.int32)[:, None]
    dispatch = at_slot.astype(jnp.bfloat16)
    combine = jnp.where(at_slot, member_gate[:, :, None, :], 0.0).astype(jnp.bfloat16)

    grouped = jnp.einsum(
        "sect,std->secd", dispatch, rows, preferred_element_type=jnp.float32
    ).astype(jnp.bfloat16)

    def product(a, b, weight, lo, hi):
        x = jnp.concatenate([grouped[a, lo:hi], grouped[b, lo:hi]], axis=1)
        return jnp.einsum("ecd,edh->ech", x, weight[lo:hi], preferred_element_type=jnp.float32)

    def summed(weight, near, far, lo, hi):
        got = to_section(product(near, 3, weight, lo, hi).astype(jnp.bfloat16), near)
        both = product(0, far, weight, lo, hi) + got.astype(jnp.float32)
        got = to_section(both[:, slots:].astype(jnp.bfloat16), far)
        return both[:, :slots] + got.astype(jnp.float32)

    def gated_sum(j, a, lo, hi):
        out = jnp.einsum(
            "ech,ehd->ecd", a, down_w[lo:hi], preferred_element_type=jnp.float32
        ).astype(jnp.bfloat16)
        return jnp.einsum(
            "ect,ecd->td", combine[j, lo:hi], out, preferred_element_type=jnp.float32
        )

    halfway = local_count // 2
    acts = []
    for lo, hi in ((0, halfway), (halfway, local_count)):
        gate, up = summed(gate_w, 1, 2, lo, hi), summed(up_w, 2, 1, lo, hi)
        act = (jax.nn.silu(gate) * up).astype(jnp.bfloat16)
        act1, act2 = to_section(act, 1), to_section(act, 2)
        cut = (hi - lo) // 2
        act3 = jnp.concatenate([to_section(act1[:cut], 2), to_section(act2[cut:], 1)], axis=0)
        acts.append((act, act1, act2, act3))
    blocks = [jnp.concatenate([part[j] for part in acts], axis=0) for j in range(sections)]

    def deliver(low, high, shift):
        low, high = (b.astype(jnp.bfloat16).reshape(zs, tok_count, depth) for b in (low, high))
        got = to_other_core(jnp.where(first_core, high, low))
        kept = jnp.where(first_core, low, high)
        both = (kept.astype(jnp.float32) + got.astype(jnp.float32)).astype(jnp.bfloat16)
        total = both[0].astype(jnp.float32)
        for k in range(1, zs):
            total = total + to_lower(both[k], k).astype(jnp.float32)
        moves = []
        for s in range(sections):
            for p in range(pairs):
                moves.append((s * pairs + p, (s ^ (shift + 2 * p)) * pairs + s // 2))
        return lax.ppermute(total.astype(jnp.bfloat16), ("section", "pair"), moves)

    block0, block1, block2, block3 = (gated_sum(j, blocks[j], 0, local_count) for j in range(sections))
    same = deliver(block0, block2, 0)
    unlike = deliver(block1, block3, 1)
    moe = jnp.where(
        me % 2 == 0,
        jnp.concatenate([same, unlike], axis=1),
        jnp.concatenate([unlike, same], axis=1),
    )
    state = lax.dynamic_slice_in_dim(mixed, pair_pos * part_width, part_width, 1)
    return (state + moe.astype(jnp.float32)).astype(jnp.bfloat16)


def on_device(initial_state, prelude, inject_gain, norm_gain, router, gate_w, up_w, down_w, routes):
    sections, zs, pairs = (lax.axis_size(a) for a in ("section", "expert", "pair"))
    slot_bytes = 2 * sections * gate_w.shape[0] * CAP * zs * zs * initial_state.shape[0]
    fits = slot_bytes <= 16 * 2**20 and sections == 4 and pairs == 2
    plan = move_tokens if fits else gather_weights
    return plan(
        initial_state, prelude, inject_gain, norm_gain, router, gate_w, up_w, down_w, routes
    )


def solution(mesh):
    placed = (
        P(("section", "expert"), None),
        P(("section", "expert"), None),
        P(),
        P(),
        P(),
        P("expert", "section", "pair"),
        P("expert", "section", "pair"),
        P("expert", "pair", "section"),
        P(None, ("section", "expert"), None),
    )
    return jax.shard_map(
        on_device,
        mesh=mesh,
        in_specs=placed,
        out_specs=P(("section", "expert"), "pair"),
        check_vma=False,
    )
```

```python
import jax
import jax.numpy as jnp
from jax import lax
from jax.sharding import PartitionSpec as P

TOPK = 8
CAP = 18


def gather_weights(initial_state, prelude, inject_gain, norm_gain, router, gate_w, up_w, down_w, routes):
    gate_full, up_full, down_full = (
        lax.all_gather(gate_w, "section", axis=1, tiled=True),
        lax.all_gather(up_w, "section", axis=1, tiled=True),
        lax.all_gather(down_w, "section", axis=2, tiled=True),
    )
    paired_w = jnp.concatenate([gate_full, up_full], axis=2)
    local_count = gate_full.shape[0]
    half_width = gate_full.shape[2]
    tok_count, model_width = initial_state.shape
    experts_all = router.shape[1]
    pair_count = lax.axis_size("pair")
    pair_pos = lax.axis_index("pair")
    part_width = model_width // pair_count
    hidden_state = initial_state.astype(jnp.float32)
    prelude_f = prelude.astype(jnp.float32)
    token_ids = jnp.broadcast_to(
        jnp.arange(tok_count, dtype=jnp.int32)[:, None], (tok_count, TOPK)
    ).reshape(-1)
    expert_range = jnp.arange(experts_all, dtype=jnp.int32)
    mixed_state = hidden_state + prelude_f * inject_gain
    inv_rms = lax.rsqrt(jnp.mean(mixed_state * mixed_state, axis=-1, keepdims=True) + 1e-06)
    normed = (mixed_state * inv_rms * norm_gain).astype(jnp.bfloat16)
    logits = jnp.dot(normed, router, preferred_element_type=jnp.float32)
    router_prob = jax.nn.sigmoid(logits)
    chosen = routes[0]
    onehot_k = (chosen[:, :, None] == expert_range).astype(jnp.float32)
    picked = jnp.sum(onehot_k * router_prob[:, None, :], axis=-1)
    gate_vals = picked / jnp.sum(picked, axis=1, keepdims=True)
    flat_ids = chosen.reshape(-1)
    onehot = (flat_ids[:, None] == expert_range).astype(jnp.bfloat16)
    order = jnp.arange(flat_ids.shape[0], dtype=jnp.int32)
    earlier = (order[:, None] > order[None, :]).astype(jnp.bfloat16)
    before = jnp.dot(earlier, onehot, preferred_element_type=jnp.float32)
    slot_rank = jnp.sum(before * onehot.astype(jnp.float32), axis=-1).astype(jnp.int32)
    slot_ids = flat_ids * CAP + slot_rank
    source_rows = jnp.full((experts_all * CAP,), tok_count, jnp.int32).at[slot_ids].set(token_ids)
    padded_rows = jnp.concatenate([normed, jnp.zeros((1, model_width), jnp.bfloat16)], axis=0)
    outgoing = padded_rows[source_rows].reshape(experts_all, CAP, padded_rows.shape[1])
    received = lax.all_to_all(outgoing, "expert", split_axis=0, concat_axis=0, tiled=True)
    slot_count = received.shape[1]
    grouped = received.reshape(-1, local_count, slot_count, model_width)
    gate_up = jnp.einsum("sekd,edh->sekh", grouped, paired_w, preferred_element_type=jnp.float32)
    inner_act = (jax.nn.silu(gate_up[..., :half_width]) * gate_up[..., half_width:]).astype(
        jnp.bfloat16
    )
    partial_out = jnp.einsum(
        "sekh,ehd->sekd", inner_act, down_full, preferred_element_type=jnp.float32
    ).astype(jnp.bfloat16)
    lead = partial_out.shape[0]
    pieces = jnp.moveaxis(
        partial_out.reshape(lead, local_count, slot_count, pair_count, part_width), 3, 0
    )
    arrived = lax.all_to_all(pieces, "pair", split_axis=0, concat_axis=0, tiled=True)
    summed = jnp.sum(arrived.astype(jnp.float32), axis=0).astype(jnp.bfloat16)
    returned_rows = lax.all_to_all(
        summed.reshape(-1, slot_count, summed.shape[-1]),
        "expert",
        split_axis=0,
        concat_axis=0,
        tiled=True,
    )
    back_width = returned_rows.shape[-1]
    flat_back = returned_rows.reshape(experts_all * CAP, back_width)
    taken_rows = flat_back[slot_ids].reshape(tok_count, TOPK, back_width)
    moe_out = jnp.sum(gate_vals[:, :, None] * taken_rows.astype(jnp.float32), axis=1)
    hidden_state = (
        lax.dynamic_slice_in_dim(mixed_state, pair_pos * part_width, part_width, 1) + moe_out
    )
    return hidden_state.astype(jnp.bfloat16)


def move_tokens(initial_state, prelude, inject_gain, norm_gain, router, gate_w, up_w, down_w, routes):
    sections, zs, pairs = (lax.axis_size(a) for a in ("section", "expert", "pair"))
    me, z, pair_pos = (lax.axis_index(a) for a in ("section", "expert", "pair"))
    local_count, depth, _ = gate_w.shape
    tok_count, model_width = initial_state.shape
    experts_all = router.shape[1]
    part_width = model_width // pairs
    slots = CAP * zs
    sec_toks = zs * tok_count
    half_toks = tok_count // pairs
    first_core = pair_pos == 0

    def to_section(x, j):
        return lax.ppermute(x, "section", [(s, s ^ j) for s in range(sections)])

    def to_lower(x, k):
        return lax.ppermute(x, "expert", [(i, (i - k) % zs) for i in range(zs)])

    def to_upper(x, k):
        return lax.ppermute(x, "expert", [(i, (i + k) % zs) for i in range(zs)])

    def to_other_core(x):
        return lax.ppermute(x, "pair", [(0, 1), (1, 0)])

    mixed = initial_state.astype(jnp.float32) + prelude.astype(jnp.float32) * inject_gain
    inv_rms = lax.rsqrt(jnp.mean(mixed * mixed, axis=-1, keepdims=True) + 1e-06)
    normed = (mixed * inv_rms * norm_gain).astype(jnp.bfloat16)

    mine = lax.dynamic_slice_in_dim(normed, pair_pos * half_toks, half_toks, 0)
    sliced = []
    for j in range(sections):
        piece = lax.dynamic_slice_in_dim(mine, (me ^ j) * depth, depth, 1)
        sliced.append(piece if j == 0 else to_section(piece, j))
    sliced = jnp.stack(sliced)
    logits = jnp.dot(normed, router, preferred_element_type=jnp.float32)
    prob = jax.nn.sigmoid(logits)
    onehot_k = (routes[0][:, :, None] == jnp.arange(experts_all, dtype=jnp.int32)).astype(jnp.float32)
    picked = jnp.sum(onehot_k * prob[:, None, :], axis=-1)
    gates = picked / jnp.sum(picked, axis=1, keepdims=True)
    table = jnp.concatenate([routes[0].astype(jnp.float32), gates], axis=1).T
    table = jnp.stack([table if j == 0 else to_section(table, j) for j in range(sections)])
    sliced, table = lax.optimization_barrier((sliced, table))
    half = jnp.stack([sliced if k == 0 else to_upper(sliced, k) for k in range(zs)], axis=1)
    other = to_other_core(half)
    rows = jnp.where(
        first_core, jnp.stack([half, other], axis=2), jnp.stack([other, half], axis=2)
    ).reshape(sections, sec_toks, depth)
    table = jnp.stack([table if k == 0 else to_upper(table, k) for k in range(zs)], axis=1)
    table = table.transpose(0, 1, 3, 2).reshape(sections, sec_toks, 2 * TOPK)
    all_routes, all_gates = table[..., :TOPK].astype(jnp.int32), table[..., TOPK:]

    own = z * local_count + jnp.arange(local_count, dtype=jnp.int32)
    hits = all_routes[:, None, :, :] == own[None, :, None, None]
    member = jnp.any(hits, axis=-1)
    member_gate = jnp.sum(jnp.where(hits, all_gates[:, None, :, :], 0.0), axis=-1)
    order = jnp.arange(sec_toks, dtype=jnp.int32)
    earlier = (order[:, None] < order[None, :]).astype(jnp.bfloat16)
    rank = jnp.einsum(
        "seu,ut->set", member.astype(jnp.bfloat16), earlier, preferred_element_type=jnp.float32
    )
    place = jnp.where(member, rank, -1.0).astype(jnp.int32)
    at_slot = place[:, :, None, :] == jnp.arange(slots, dtype=jnp.int32)[:, None]
    dispatch = at_slot.astype(jnp.bfloat16)
    combine = jnp.where(at_slot, member_gate[:, :, None, :], 0.0).astype(jnp.bfloat16)

    grouped = jnp.einsum(
        "sect,std->secd", dispatch, rows, preferred_element_type=jnp.float32
    ).astype(jnp.bfloat16)

    def product(a, b, weight, lo, hi):
        x = jnp.concatenate([grouped[a, lo:hi], grouped[b, lo:hi]], axis=1)
        return jnp.einsum("ecd,edh->ech", x, weight[lo:hi], preferred_element_type=jnp.float32)

    def summed(weight, near, far, lo, hi):
        got = to_section(product(near, 3, weight, lo, hi).astype(jnp.bfloat16), near)
        both = product(0, far, weight, lo, hi) + got.astype(jnp.float32)
        got = to_section(both[:, slots:].astype(jnp.bfloat16), far)
        return both[:, :slots] + got.astype(jnp.float32)

    def gated_sum(j, a, lo, hi):
        out = jnp.einsum(
            "ech,ehd->ecd", a, down_w[lo:hi], preferred_element_type=jnp.float32
        ).astype(jnp.bfloat16)
        return jnp.einsum(
            "ect,ecd->td", combine[j, lo:hi], out, preferred_element_type=jnp.float32
        )

    halfway = local_count // 2
    acts = []
    for lo, hi in ((0, halfway), (halfway, local_count)):
        gate, up = summed(gate_w, 1, 2, lo, hi), summed(up_w, 2, 1, lo, hi)
        act = (jax.nn.silu(gate) * up).astype(jnp.bfloat16)
        act1, act2 = to_section(act, 1), to_section(act, 2)
        cut = (hi - lo) // 2
        act3 = jnp.concatenate([to_section(act1[:cut], 2), to_section(act2[cut:], 1)], axis=0)
        acts.append((act, act1, act2, act3))
    blocks = [jnp.concatenate([part[j] for part in acts], axis=0) for j in range(sections)]

    def deliver(low, high, shift):
        low, high = (b.astype(jnp.bfloat16).reshape(zs, tok_count, depth) for b in (low, high))
        got = to_other_core(jnp.where(first_core, high, low))
        kept = jnp.where(first_core, low, high)
        both = (kept.astype(jnp.float32) + got.astype(jnp.float32)).astype(jnp.bfloat16)
        total = both[0].astype(jnp.float32)
        for k in range(1, zs):
            total = total + to_lower(both[k], k).astype(jnp.float32)
        moves = []
        for s in range(sections):
            for p in range(pairs):
                moves.append((s * pairs + p, (s ^ (shift + 2 * p)) * pairs + s // 2))
        return lax.ppermute(total.astype(jnp.bfloat16), ("section", "pair"), moves)

    block0, block1, block2, block3 = (gated_sum(j, blocks[j], 0, local_count) for j in range(sections))
    same = deliver(block0, block2, 0)
    unlike = deliver(block1, block3, 1)
    moe = jnp.where(
        me % 2 == 0,
        jnp.concatenate([same, unlike], axis=1),
        jnp.concatenate([unlike, same], axis=1),
    )
    state = lax.dynamic_slice_in_dim(mixed, pair_pos * part_width, part_width, 1)
    return (state + moe.astype(jnp.float32)).astype(jnp.bfloat16)


def on_device(initial_state, prelude, inject_gain, norm_gain, router, gate_w, up_w, down_w, routes):
    sections, zs, pairs = (lax.axis_size(a) for a in ("section", "expert", "pair"))
    slot_bytes = 2 * sections * gate_w.shape[0] * CAP * zs * zs * initial_state.shape[0]
    fits = slot_bytes <= 16 * 2**20 and sections == 4 and pairs == 2
    plan = move_tokens if fits else gather_weights
    return plan(
        initial_state, prelude, inject_gain, norm_gain, router, gate_w, up_w, down_w, routes
    )


def solution(mesh):
    placed = (
        P(("section", "expert"), None),
        P(("section", "expert"), None),
        P(),
        P(),
        P(),
        P("expert", "section", "pair"),
        P("expert", "section", "pair"),
        P("expert", "pair", "section"),
        P(None, ("section", "expert"), None),
    )
    return jax.shard_map(
        on_device,
        mesh=mesh,
        in_specs=placed,
        out_specs=P(("section", "expert"), "pair"),
        check_vma=False,
    )
```
